32 devices in a mesh: freq: 4 (over x, core), pos: 8 (over z, y).
Axes of the slice: x: 2, y: 2, z: 4, core: 2. Of those that a mesh axis runs over, the one named last changes fastest.
Arguments:
- spectra: bfloat16 [16, 2, 256, 8192], P(None, None, 'freq', 'pos'), may hold values from -6 to 6
- green: bfloat16 [16, 8192, 2048], P('freq', 'pos'), may hold values from -0.046875 to 0.046875
- recorded: bfloat16 [256, 1024, 512], P('pos', 'freq'), may hold values from -6 to 6
- filter_taps: float32 [256, 11], P('pos'), may hold values from -3 to 3
Outputs:
- primaries: bfloat16 [256, 1024, 512], P('pos', 'freq')
The draws below stay inside these ranges and needn't reach their ends.
All inputs are finite; a program needn't handle non-finite values.
Results may differ from the reference program's by a relative error of at most 0.001.
Values may be sent and summed in bfloat16 or wider, within the bound.
A program may use at most 128 MiB of HBM per device.

```python
import jax
import jax.numpy as jnp
from jax import lax

S = 256
R = 1024
NT = 512
TAPS = 11
BAND_START = 32
K = 8192
F = 16


def spiked(entries, key, source, target, shards_of, factor):
    owner, partner = [(jnp.arange(entries.shape[position]) // (entries.shape[position] // shards_of)).reshape([-1 if axis == position else 1 for axis in range(entries.ndim)]) for position in (source, target)]
    chosen = jax.random.permutation(key, shards_of)[partner]
    strong = (owner == chosen) | (owner == (partner + shards_of // 2) % shards_of)
    return jnp.where(strong, factor * entries, entries)


def block_levels(stream_key, dims, cuts, low, high):
    gain, own = 1.0, jax.random.fold_in(stream_key, 6)
    for position, parts in cuts:
        steps = jnp.exp(jax.random.uniform(jax.random.fold_in(own, position), (parts,), jnp.float32, low / len(cuts), high / len(cuts)))
        gain = gain * jnp.repeat(steps, dims[position] // parts).reshape([-1 if axis == position else 1 for axis in range(len(dims))])
    return gain


def centred(rng, shape, deviation, most, split=(), kind=jnp.bfloat16):
    level = block_levels(rng, shape, split, -0.22, 0.18) if split else 1.0
    drawn = jax.random.normal(rng, shape, jnp.float32) * deviation * level
    return jnp.minimum(jnp.maximum(drawn, -most), most).astype(kind)


def bell_draw_with(key, shape, deviation, limit, split, heavy, kind=jnp.bfloat16):
    entries = deviation * jax.random.normal(key, shape, jnp.float32)
    if split:
        entries = entries * block_levels(key, shape, split, -0.22, 0.18)
    return jnp.clip(spiked(entries, jax.random.fold_in(key, 3), *heavy), -limit, limit).astype(kind)


def setup_inputs(seed: int = 0) -> dict:
    key_of = jax.random.split(jax.random.key(seed), 5)
    spectra = bell_draw_with(key_of[0], (F, 2, S, K), 1.0, 6.0, ((2, 4), (3, 8)), (3, 2, 8, 2.0))
    green = centred(key_of[1], (F, K, 2 * R), (2 * K) ** -0.5, 0.046875, ((0, 4), (1, 8)))
    recorded = centred(key_of[2], (S, R, NT), 1.0, 6.0, ((0, 8), (1, 4)))
    filter_taps = centred(key_of[3], (S, TAPS), 0.3, 3.0, ((0, 8),), jnp.float32)
    return dict(spectra=spectra, green=green, recorded=recorded, filter_taps=filter_taps)


def phase_table(first_freq, freq_count, total_freqs, samples):
    bins = BAND_START + first_freq + jnp.arange(freq_count, dtype=jnp.int32)
    sample_index = jnp.arange(samples, dtype=jnp.int32)
    phase = bins[:, None] * sample_index[None, :] % samples
    angle = 2.0 * jnp.pi / samples * phase.astype(jnp.float32)
    scale = 1.0 / jnp.sqrt(jnp.float32(total_freqs))
    return jnp.stack([jnp.cos(angle), -jnp.sin(angle)], 1) * scale

def reference(spectra, green, recorded, filter_taps):

    def one_slice(pair):
        slice_spectra, slice_green = pair
        product = jnp.dot(slice_spectra.reshape(2 * S, K), slice_green, preferred_element_type=jnp.float32)
        real_part = product[:S, :R] - product[S:, R:]
        imag_part = product[:S, R:] + product[S:, :R]
        return jnp.stack([real_part, imag_part], 0)
    prediction = lax.map(one_slice, (spectra, green))
    table = phase_table(0, F, F, NT)
    predicted = jnp.einsum('fisr,fit->srt', prediction, table, precision=lax.Precision.HIGHEST)
    margin = (TAPS - 1) // 2
    padded = jnp.pad(predicted, ((0, 0), (0, 0), (margin, margin)))
    result = recorded.astype(jnp.float32)
    for lag in range(TAPS):
        result = result - filter_taps[:, lag][:, None, None] * padded[:, :, lag:lag + NT]
    return result.astype(jnp.bfloat16)
```

```python
import functools

import jax
import jax.numpy as jnp
from jax import lax
from jax.experimental import pallas as pl
from jax.experimental.pallas import tpu as pltpu
from jax.sharding import PartitionSpec as P

BAND_START = 32
MESH = pl.DeviceIdType.MESH
TINY = 2.0**-126
Y_LAG = 2
Z_LAG = 4
AHEAD = 2


def phase_table(first_freq, freq_count, total_freqs, samples):
    bins = BAND_START + first_freq + jnp.arange(freq_count, dtype=jnp.int32)
    sample_index = jnp.arange(samples, dtype=jnp.int32)
    phase = bins[:, None] * sample_index[None, :] % samples
    angle = 2.0 * jnp.pi / samples * phase.astype(jnp.float32)
    scale = 1.0 / jnp.sqrt(jnp.float32(total_freqs))
    return jnp.stack([jnp.cos(angle), -jnp.sin(angle)], 1) * scale


def encode(x):
    x2 = (x * x) * 16.0
    x4 = x2 * x2
    y = x4 * x4
    return jnp.where(x < 0, -y, y).astype(jnp.bfloat16)


def decode(code):
    y = code.astype(jnp.float32)
    half = lax.rsqrt(jnp.maximum(jnp.abs(y), TINY))
    quarter = lax.rsqrt(half)
    size = lax.rsqrt(quarter) * quarter * 0.25
    return jnp.where(y < 0, -size, size)


def gather_kernel(
    nq, npos, spectra, green, out, xs, gbuf, acc, keep, ysend, yrecv, zsend, zrecv, fin, finrecv,
    xss, xrs, xls, gs, yss, yrs, zss, zrs, fss, frs,
):
    floc = green.shape[0]
    shots = spectra.shape[2]
    depth = spectra.shape[3]
    half_cols = green.shape[2] // 2
    width = half_cols // nq
    own = shots * nq // npos
    line = npos // 2
    chunks = floc * nq
    q = lax.axis_index("freq")
    p = lax.axis_index("pos")
    y = lax.rem(p, 2)
    z = p // 2
    other = p + 1 - 2 * y

    def turn(start, step, size):
        return lax.rem(start + step, size)

    barrier = pltpu.get_barrier_semaphore()
    for d in range(1, nq):
        pl.semaphore_signal(barrier, inc=1, device_id={"freq": turn(q, d, nq)}, device_id_type=MESH)
    pl.semaphore_signal(barrier, inc=1, device_id={"pos": other}, device_id_type=MESH)
    for d in range(1, line):
        pl.semaphore_signal(
            barrier, inc=1, device_id={"pos": turn(z, d, line) * 2 + y}, device_id_type=MESH
        )
    pl.semaphore_wait(barrier, nq - 1 + 1 + line - 1)

    def green_copy(f):
        return pltpu.make_async_copy(green.at[f], gbuf.at[lax.rem(f, 2)], gs.at[lax.rem(f, 2)])

    def own_spectra(f):
        return pltpu.make_async_copy(spectra.at[q * floc + f], xs.at[f, q], xls.at[f])

    def send_spectra(f, target):
        return pltpu.make_async_remote_copy(
            src_ref=spectra.at[target * floc + f],
            dst_ref=xs.at[f, q],
            send_sem=xss.at[f, target],
            recv_sem=xrs.at[f, q],
            device_id={"freq": target},
            device_id_type=MESH,
        )

    def recv_spectra(f, source):
        return pltpu.make_async_remote_copy(
            src_ref=spectra.at[q * floc + f],
            dst_ref=xs.at[f, source],
            send_sem=xss.at[f, source],
            recv_sem=xrs.at[f, source],
            device_id={"freq": source},
            device_id_type=MESH,
        )

    def start_spectra(f):
        for d in (2, 1, 3) if nq == 4 else range(1, nq):
            send_spectra(f, turn(q, d, nq)).start()

    def y_copy(n):
        return pltpu.make_async_remote_copy(
            src_ref=ysend.at[n],
            dst_ref=yrecv.at[n],
            send_sem=yss.at[n],
            recv_sem=yrs.at[n],
            device_id={"pos": other},
            device_id_type=MESH,
        )

    def z_copy(n, there, slot):
        return pltpu.make_async_remote_copy(
            src_ref=zsend.at[n, there],
            dst_ref=zrecv.at[n, slot],
            send_sem=zss.at[n, there],
            recv_sem=zrs.at[n, slot],
            device_id={"pos": there * 2 + y},
            device_id_type=MESH,
        )

    def fin_copy(f, there, slot):
        return pltpu.make_async_remote_copy(
            src_ref=fin.at[f, there],
            dst_ref=finrecv.at[slot, f],
            send_sem=fss.at[f, there],
            recv_sem=frs.at[slot, f],
            device_id={"freq": there},
            device_id_type=MESH,
        )

    for f in range(min(AHEAD, floc)):
        start_spectra(f)
    for f in range(floc):
        own_spectra(f).start()
    for f in range(min(2, floc)):
        green_copy(f).start()

    def multiply(n):
        f = n // nq
        d = lax.rem(n, nq)
        col = turn(q, d + 1, nq)

        @pl.when(d == 0)
        def _():
            own_spectra(f).wait()
            for step in range(1, nq):
                recv_spectra(f, turn(q, step, nq)).wait_recv()

            @pl.when(f + AHEAD < floc)
            def _():
                start_spectra(f + AHEAD)

            green_copy(f).wait()

            @pl.when((f >= 1) & (f + 1 < floc))
            def _():
                green_copy(f + 1).start()

        left = xs[f].reshape(nq * 2 * shots, depth)
        slot = lax.rem(f, 2)
        for part in range(2):
            columns = pl.ds(pl.multiple_of(part * half_cols + col * width, 128), width)
            acc[part] = jnp.dot(left, gbuf[slot, :, columns], preferred_element_type=jnp.float32)

        for there in range(line):
            for mine in (True, False):
                shot = (there * 2 + (y if mine else 1 - y)) * own
                row = (shot // shots) * (2 * shots) + lax.rem(shot, shots)
                re_rows = pl.ds(pl.multiple_of(row, 16), own)
                im_rows = pl.ds(pl.multiple_of(row + shots, 16), own)
                real = acc[0, re_rows] - acc[1, im_rows]
                imag = acc[1, re_rows] + acc[0, im_rows]
                if mine:
                    keep[n, there, 0] = real
                    keep[n, there, 1] = imag
                else:
                    ysend[n, there, 0] = encode(real)
                    ysend[n, there, 1] = encode(imag)
        y_copy(n).start()

    def pair(n):
        y_copy(n).wait_recv()
        for d in range(1, line):
            there = turn(z, d, line)
            zsend[n, there] = encode(keep[n, there] + decode(yrecv[n, there]))
            z_copy(n, there, z).start()
        keep[n, z] = keep[n, z] + decode(yrecv[n, z])

    def finish(n):
        f = n // nq
        d = lax.rem(n, nq)
        col = turn(q, d + 1, nq)
        total = keep[n, z]
        for step in range(1, line):
            source = turn(z, step, line)
            z_copy(n, source, source).wait_recv()
            total = total + decode(zrecv[n, source])

        @pl.when(d == nq - 1)
        def _():
            finrecv[q, f] = total

        @pl.when(d < nq - 1)
        def _():
            fin[f, col] = total
            fin_copy(f, col, q).start()

    def step(n, carry):
        @pl.when(n < chunks)
        def _():
            multiply(n)

        @pl.when((n >= Y_LAG) & (n < chunks + Y_LAG))
        def _():
            pair(n - Y_LAG)

        @pl.when(n >= Z_LAG)
        def _():
            finish(n - Z_LAG)

        return carry

    lax.fori_loop(0, chunks + Z_LAG, step, 0)

    def wait_sends(n, carry):
        y_copy(n).wait_send()
        for d in range(1, line):
            z_copy(n, turn(z, d, line), z).wait_send()
        return carry

    lax.fori_loop(0, chunks, wait_sends, 0)

    def wait_freq(f, carry):
        for d in range(1, nq):
            peer = turn(q, d, nq)
            send_spectra(f, peer).wait_send()
            fin_copy(f, peer, q).wait_send()
            fin_copy(f, peer, peer).wait_recv()
        return carry

    lax.fori_loop(0, floc, wait_freq, 0)
    out[...] = finrecv[...]


def gathered(spectra, green, nq, npos):
    total, _, shots, depth = spectra.shape
    floc = green.shape[0]
    half_cols = green.shape[2] // 2
    width = half_cols // nq
    own = shots * nq // npos
    line = npos // 2
    chunks = floc * nq
    f32, bf16 = jnp.float32, jnp.bfloat16
    dma = pltpu.SemaphoreType.DMA
    return pl.pallas_call(
        functools.partial(gather_kernel, nq, npos),
        out_shape=jax.ShapeDtypeStruct((nq, floc, 2, own, width), f32),
        in_specs=[pl.BlockSpec(memory_space=pl.ANY)] * 2,
        out_specs=pl.BlockSpec(memory_space=pltpu.VMEM),
        scratch_shapes=[
            pltpu.VMEM((floc, nq, 2, shots, depth), bf16),
            pltpu.VMEM((2, depth, 2 * half_cols), bf16),
            pltpu.VMEM((2, nq * 2 * shots, width), f32),
            pltpu.VMEM((chunks, line, 2, own, width), f32),
            pltpu.VMEM((chunks, line, 2, own, width), bf16),
            pltpu.VMEM((chunks, line, 2, own, width), bf16),
            pltpu.VMEM((chunks, line, 2, own, width), bf16),
            pltpu.VMEM((chunks, line, 2, own, width), bf16),
            pltpu.VMEM((floc, nq, 2, own, width), f32),
            pltpu.VMEM((nq, floc, 2, own, width), f32),
            dma((floc, nq)),
            dma((floc, nq)),
            dma((floc,)),
            dma((2,)),
            dma((chunks,)),
            dma((chunks,)),
            dma((chunks, line)),
            dma((chunks, line)),
            dma((floc, nq)),
            dma((nq, floc)),
        ],
        compiler_params=pltpu.CompilerParams(
            collective_id=0, has_side_effects=True, vmem_limit_bytes=56 * 2**20
        ),
        name="gather_sum",
    )(spectra, green)


def subtract_kernel(pred, table, recorded, out):
    swapped = jnp.swapaxes(pred[...], 0, 1)
    for s in range(out.shape[0]):
        value = swapped[s]
        top = value.astype(jnp.bfloat16)
        low = (value - top.astype(jnp.float32)).astype(jnp.bfloat16)
        wave = table[s]
        wave_top = wave.astype(jnp.bfloat16)
        wave_low = (wave - wave_top.astype(jnp.float32)).astype(jnp.bfloat16)
        left = jnp.concatenate([top, top, low], 0)
        right = jnp.concatenate([wave_top, wave_low, wave_top], 0)
        filtered = lax.dot_general(
            left, right, (((0,), (0,)), ((), ())), preferred_element_type=jnp.float32
        )
        out[s] = (recorded[s].astype(jnp.float32) - filtered).astype(jnp.bfloat16)


def subtract(pred, table, recorded):
    rows, own, width = pred.shape
    samples = recorded.shape[2]
    group = 8
    return pl.pallas_call(
        subtract_kernel,
        out_shape=jax.ShapeDtypeStruct(recorded.shape, jnp.bfloat16),
        grid=(own // group,),
        in_specs=[
            pl.BlockSpec((rows, group, width), lambda i: (0, i, 0)),
            pl.BlockSpec((group, rows, samples), lambda i: (i, 0, 0)),
            pl.BlockSpec((group, width, samples), lambda i: (i, 0, 0)),
        ],
        out_specs=pl.BlockSpec((group, width, samples), lambda i: (i, 0, 0)),
        compiler_params=pltpu.CompilerParams(vmem_limit_bytes=48 * 2**20),
        name="subtract",
    )(pred, table, recorded)


def on_device(nq, npos, spectra, green, recorded, filter_taps):
    samples = recorded.shape[2]
    total_freqs = spectra.shape[0]
    tap_count = filter_taps.shape[1]
    margin = (tap_count - 1) // 2
    table = phase_table(0, total_freqs, total_freqs, samples).reshape(2 * total_freqs, samples)
    padded = jnp.pad(table, ((0, 0), (margin, margin)))
    shifted = jnp.stack([padded[:, lag : lag + samples] for lag in range(tap_count)])
    waves = jnp.einsum("sl,lft->sft", filter_taps, shifted, precision=lax.Precision.HIGHEST)
    share = gathered(spectra, green, nq, npos)
    pred = share.reshape(2 * total_freqs, share.shape[3], share.shape[4])
    return subtract(pred, waves, recorded)


def solution(mesh):
    placed = (
        P(None, None, "freq", "pos"),
        P("freq", "pos", None),
        P("pos", "freq", None),
        P("pos", None),
    )
    return jax.shard_map(
        functools.partial(on_device, mesh.shape["freq"], mesh.shape["pos"]),
        mesh=mesh,
        in_specs=placed,
        out_specs=P("pos", "freq", None),
        check_vma=False,
    )
```

```python
import functools

import jax
import jax.numpy as jnp
import numpy as np
from jax import lax
from jax.experimental import pallas as pl
from jax.experimental.pallas import tpu as pltpu
from jax.sharding import PartitionSpec as P

BAND_START = 32
MESH = pl.DeviceIdType.MESH
TINY = 2.0**-126
Y_LAG = 2
Z_LAG = 4
AHEAD = 2


def phase_table(first_freq, freq_count, total_freqs, samples):
    bins = BAND_START + first_freq + np.arange(freq_count)
    phase = bins[:, None] * np.arange(samples)[None, :] % samples
    angle = 2.0 * np.pi / samples * phase
    return (np.stack([np.cos(angle), -np.sin(angle)], 1) / np.sqrt(total_freqs)).astype(np.float32)


def encode(x):
    x2 = (x * x) * 16.0
    x4 = x2 * x2
    y = x4 * x4
    return jnp.where(x < 0, -y, y).astype(jnp.bfloat16)


def decode(code):
    y = code.astype(jnp.float32)
    half = lax.rsqrt(jnp.maximum(jnp.abs(y), TINY))
    quarter = lax.rsqrt(half)
    size = lax.rsqrt(quarter) * quarter * 0.25
    return jnp.where(y < 0, -size, size)


def gather_kernel(
    nq, npos, spectra, green, taps, shifted, out, waves, xs, gbuf, acc, keep, ysend, yrecv, zsend, zrecv, fin, finrecv,
    xss, xrs, xls, gs, yss, yrs, zss, zrs, fss, frs,
):
    floc = green.shape[0]
    shots = spectra.shape[2]
    depth = spectra.shape[3]
    half_cols = green.shape[2] // 2
    width = half_cols // nq
    own = shots * nq // npos
    line = npos // 2
    chunks = floc * nq
    q = lax.axis_index("freq")
    p = lax.axis_index("pos")
    y = lax.rem(p, 2)
    z = p // 2
    other = p + 1 - 2 * y

    def turn(start, step, size):
        return lax.rem(start + step, size)

    barrier = pltpu.get_barrier_semaphore()
    for d in range(1, nq):
        pl.semaphore_signal(barrier, inc=1, device_id={"freq": turn(q, d, nq)}, device_id_type=MESH)
    pl.semaphore_signal(barrier, inc=1, device_id={"pos": other}, device_id_type=MESH)
    for d in range(1, line):
        pl.semaphore_signal(
            barrier, inc=1, device_id={"pos": turn(z, d, line) * 2 + y}, device_id_type=MESH
        )
    pl.semaphore_wait(barrier, nq - 1 + 1 + line - 1)

    def green_copy(f):
        return pltpu.make_async_copy(green.at[f], gbuf.at[lax.rem(f, 2)], gs.at[lax.rem(f, 2)])

    def own_spectra(f):
        return pltpu.make_async_copy(spectra.at[q * floc + f], xs.at[f, q], xls.at[f])

    def send_spectra(f, target):
        return pltpu.make_async_remote_copy(
            src_ref=spectra.at[target * floc + f],
            dst_ref=xs.at[f, q],
            send_sem=xss.at[f, target],
            recv_sem=xrs.at[f, q],
            device_id={"freq": target},
            device_id_type=MESH,
        )

    def recv_spectra(f, source):
        return pltpu.make_async_remote_copy(
            src_ref=spectra.at[q * floc + f],
            dst_ref=xs.at[f, source],
            send_sem=xss.at[f, source],
            recv_sem=xrs.at[f, source],
            device_id={"freq": source},
            device_id_type=MESH,
        )

    def start_spectra(f):
        for d in (2, 1, 3) if nq == 4 else range(1, nq):
            send_spectra(f, turn(q, d, nq)).start()

    def y_copy(n):
        return pltpu.make_async_remote_copy(
            src_ref=ysend.at[n],
            dst_ref=yrecv.at[n],
            send_sem=yss.at[n],
            recv_sem=yrs.at[n],
            device_id={"pos": other},
            device_id_type=MESH,
        )

    def z_copy(n, there, slot):
        return pltpu.make_async_remote_copy(
            src_ref=zsend.at[n, there],
            dst_ref=zrecv.at[n, slot],
            send_sem=zss.at[n, there],
            recv_sem=zrs.at[n, slot],
            device_id={"pos": there * 2 + y},
            device_id_type=MESH,
        )

    def fin_copy(f, there, slot):
        return pltpu.make_async_remote_copy(
            src_ref=fin.at[f, there],
            dst_ref=finrecv.at[slot, f],
            send_sem=fss.at[f, there],
            recv_sem=frs.at[slot, f],
            device_id={"freq": there},
            device_id_type=MESH,
        )

    for f in range(min(AHEAD, floc)):
        start_spectra(f)
    for f in range(floc):
        own_spectra(f).start()
    for f in range(min(2, floc)):
        green_copy(f).start()

    def wave(s, carry):
        total = taps[0, s] * shifted[0]
        for lag in range(1, shifted.shape[0]):
            total = total + taps[lag, s] * shifted[lag]
        top = total.astype(jnp.bfloat16)
        waves[s, 0] = top
        waves[s, 1] = (total - top.astype(jnp.float32)).astype(jnp.bfloat16)
        return carry

    lax.fori_loop(0, own, wave, 0)

    def multiply(n):
        f = n // nq
        d = lax.rem(n, nq)
        col = turn(q, d + 1, nq)

        @pl.when(d == 0)
        def _():
            own_spectra(f).wait()
            for step in range(1, nq):
                recv_spectra(f, turn(q, step, nq)).wait_recv()

            @pl.when(f + AHEAD < floc)
            def _():
                start_spectra(f + AHEAD)

            green_copy(f).wait()

            @pl.when((f >= 1) & (f + 1 < floc))
            def _():
                green_copy(f + 1).start()

        left = xs[f].reshape(nq * 2 * shots, depth)
        slot = lax.rem(f, 2)
        for part in range(2):
            columns = pl.ds(pl.multiple_of(part * half_cols + col * width, 128), width)
            acc[part] = jnp.dot(left, gbuf[slot, :, columns], preferred_element_type=jnp.float32)

        for there in range(line):
            for mine in (True, False):
                shot = (there * 2 + (y if mine else 1 - y)) * own
                row = (shot // shots) * (2 * shots) + lax.rem(shot, shots)
                re_rows = pl.ds(pl.multiple_of(row, 16), own)
                im_rows = pl.ds(pl.multiple_of(row + shots, 16), own)
                real = acc[0, re_rows] - acc[1, im_rows]
                imag = acc[1, re_rows] + acc[0, im_rows]
                if mine:
                    keep[n, there, 0] = real
                    keep[n, there, 1] = imag
                else:
                    ysend[n, there, 0] = encode(real)
                    ysend[n, there, 1] = encode(imag)
        y_copy(n).start()

    def pair(n):
        y_copy(n).wait_recv()
        for d in range(1, line):
            there = turn(z, d, line)
            zsend[n, there] = encode(keep[n, there] + decode(yrecv[n, there]))
            z_copy(n, there, z).start()
        keep[n, z] = keep[n, z] + decode(yrecv[n, z])

    def finish(n):
        f = n // nq
        d = lax.rem(n, nq)
        col = turn(q, d + 1, nq)
        total = keep[n, z]
        for step in range(1, line):
            source = turn(z, step, line)
            z_copy(n, source, source).wait_recv()
            total = total + decode(zrecv[n, source])

        @pl.when(d == nq - 1)
        def _():
            finrecv[q, f] = total

        @pl.when(d < nq - 1)
        def _():
            fin[f, col] = total
            fin_copy(f, col, q).start()

    def step(n, carry):
        @pl.when(n < chunks)
        def _():
            multiply(n)

        @pl.when((n >= Y_LAG) & (n < chunks + Y_LAG))
        def _():
            pair(n - Y_LAG)

        @pl.when(n >= Z_LAG)
        def _():
            finish(n - Z_LAG)

        return carry

    lax.fori_loop(0, chunks + Z_LAG, step, 0)

    def wait_sends(n, carry):
        y_copy(n).wait_send()
        for d in range(1, line):
            z_copy(n, turn(z, d, line), z).wait_send()
        return carry

    lax.fori_loop(0, chunks, wait_sends, 0)

    def wait_freq(f, carry):
        for d in range(1, nq):
            peer = turn(q, d, nq)
            send_spectra(f, peer).wait_send()
            fin_copy(f, peer, q).wait_send()
            fin_copy(f, peer, peer).wait_recv()
        return carry

    lax.fori_loop(0, floc, wait_freq, 0)
    out[...] = finrecv[...]


def gathered(spectra, green, taps, shifted, nq, npos):
    total, _, shots, depth = spectra.shape
    floc = green.shape[0]
    half_cols = green.shape[2] // 2
    width = half_cols // nq
    own = shots * nq // npos
    line = npos // 2
    chunks = floc * nq
    f32, bf16 = jnp.float32, jnp.bfloat16
    dma = pltpu.SemaphoreType.DMA
    return pl.pallas_call(
        functools.partial(gather_kernel, nq, npos),
        out_shape=(
            jax.ShapeDtypeStruct((nq, floc, 2, own, width), f32),
            jax.ShapeDtypeStruct((own, 2, *shifted.shape[1:]), bf16),
        ),
        in_specs=[
            pl.BlockSpec(memory_space=pl.ANY),
            pl.BlockSpec(memory_space=pl.ANY),
            pl.BlockSpec(memory_space=pltpu.SMEM),
            pl.BlockSpec(memory_space=pltpu.VMEM),
        ],
        out_specs=[pl.BlockSpec(memory_space=pltpu.VMEM)] * 2,
        scratch_shapes=[
            pltpu.VMEM((floc, nq, 2, shots, depth), bf16),
            pltpu.VMEM((2, depth, 2 * half_cols), bf16),
            pltpu.VMEM((2, nq * 2 * shots, width), f32),
            pltpu.VMEM((chunks, line, 2, own, width), f32),
            pltpu.VMEM((chunks, line, 2, own, width), bf16),
            pltpu.VMEM((chunks, line, 2, own, width), bf16),
            pltpu.VMEM((chunks, line, 2, own, width), bf16),
            pltpu.VMEM((chunks, line, 2, own, width), bf16),
            pltpu.VMEM((floc, nq, 2, own, width), f32),
            pltpu.VMEM((nq, floc, 2, own, width), f32),
            dma((floc, nq)),
            dma((floc, nq)),
            dma((floc,)),
            dma((2,)),
            dma((chunks,)),
            dma((chunks,)),
            dma((chunks, line)),
            dma((chunks, line)),
            dma((floc, nq)),
            dma((nq, floc)),
        ],
        compiler_params=pltpu.CompilerParams(
            collective_id=0, has_side_effects=True, vmem_limit_bytes=56 * 2**20
        ),
        name="gather_sum",
    )(spectra, green, taps, shifted)


def subtract_kernel(pred, table, recorded, out):
    swapped = jnp.swapaxes(pred[...], 0, 1)
    for s in range(out.shape[0]):
        value = swapped[s]
        top = value.astype(jnp.bfloat16)
        low = (value - top.astype(jnp.float32)).astype(jnp.bfloat16)
        wave_top = table[s, 0]
        wave_low = table[s, 1]
        left = jnp.concatenate([top, top, low], 0)
        right = jnp.concatenate([wave_top, wave_low, wave_top], 0)
        filtered = lax.dot_general(
            left, right, (((0,), (0,)), ((), ())), preferred_element_type=jnp.float32
        )
        out[s] = (recorded[s].astype(jnp.float32) - filtered).astype(jnp.bfloat16)


def subtract(pred, table, recorded):
    rows, own, width = pred.shape
    samples = recorded.shape[2]
    group = 8
    return pl.pallas_call(
        subtract_kernel,
        out_shape=jax.ShapeDtypeStruct(recorded.shape, jnp.bfloat16),
        grid=(own // group,),
        in_specs=[
            pl.BlockSpec((rows, group, width), lambda i: (0, i, 0)),
            pl.BlockSpec((group, 2, rows, samples), lambda i: (i, 0, 0, 0)),
            pl.BlockSpec((group, width, samples), lambda i: (i, 0, 0)),
        ],
        out_specs=pl.BlockSpec((group, width, samples), lambda i: (i, 0, 0)),
        compiler_params=pltpu.CompilerParams(vmem_limit_bytes=62 * 2**20),
        name="subtract",
    )(pred, table, recorded)


def on_device(nq, npos, spectra, green, recorded, filter_taps):
    samples = recorded.shape[2]
    total_freqs = spectra.shape[0]
    tap_count = filter_taps.shape[1]
    margin = (tap_count - 1) // 2
    table = phase_table(0, total_freqs, total_freqs, samples).reshape(2 * total_freqs, samples)
    padded = np.pad(table, ((0, 0), (margin, margin)))
    shifted = np.stack([padded[:, lag : lag + samples] for lag in range(tap_count)])
    share, waves = gathered(spectra, green, filter_taps.T, jnp.asarray(shifted), nq, npos)
    pred = share.reshape(2 * total_freqs, share.shape[3], share.shape[4])
    return subtract(pred, waves, recorded)


def solution(mesh):
    placed = (
        P(None, None, "freq", "pos"),
        P("freq", "pos", None),
        P("pos", "freq", None),
        P("pos", None),
    )
    return jax.shard_map(
        functools.partial(on_device, mesh.shape["freq"], mesh.shape["pos"]),
        mesh=mesh,
        in_specs=placed,
        out_specs=P("pos", "freq", None),
        check_vma=False,
    )
```
